32 devices in a mesh: shot: 2 (over x), gx: 16 (over z, y, core).
Axes of the slice: x: 2, y: 2, z: 4, core: 2. Of those that a mesh axis runs over, the one named last changes fastest.
Arguments:
- fwd_fields: float32 [6, 256, 64, 512], P(None, ('shot', 'gx')), parts along dimension 1, may hold values from -6 to 6
- velocity: float32 [128, 64, 512], P('gx'), may hold values from 1.5 to 4.4
- adj_prev: float32 [256, 64, 512], P(('shot', 'gx')), parts along dimension 0, may hold values from -8 to 20
- adj_now: float32 [256, 64, 512], P(('shot', 'gx')), parts along dimension 0, may hold values from -8 to 20
- residual: float32 [4, 8192], P(None, ('shot', 'gx')), parts along dimension 1, may hold values from -6 to 6
- rec_owner: int32 [4096, 1], P('gx'), may hold values from 0 to 15; in each aligned block of 256 rows (0 to 255, 256 to 511, ...) at most 16 rows name the same one
- rec_cell: int32 [4096], P('gx'), may hold values from 0 to 262143
- rec_cluster: int32 [4096], P('gx'), may hold values from 0 to 31
- cluster_gain: float32 [32], replicated, may hold values from 0.5 to 2
Outputs:
- adjoint_older: float32 [256, 64, 512], P(('shot', 'gx')), parts along dimension 0
- adjoint_newer: float32 [256, 64, 512], P(('shot', 'gx')), parts along dimension 0
- gradient: float32 [256, 64, 512], P(('shot', 'gx')), parts along dimension 0
The draws below stay inside these ranges and needn't reach their ends.
There are 2 independent parts, one for each index of `shot`. The reference program is written for one: setup_inputs(seed, part) draws one part's arguments, and reference() takes and returns one part's arrays. A program takes and returns all parts, laid end to end along the dimension named above; an argument that names none is the same for every part. Nothing has to cross between parts.
Inputs may be any that keep to these rules, and one draw needn't show every extreme that they name: `rec_owner`: among the traces of one device (aligned blocks of 256 rows) at most 16 name the same block; some block is named by exactly 16 of them.
All inputs are finite; a program needn't handle non-finite values.
Results may differ from the reference program's by a relative error of at most 0.00002.
Values sent between devices are 32-bit elements; how exact they have to be, the bound alone decides.
A program may use at most 64 MiB of HBM per device.

```python
import math
import jax
import jax.numpy as jnp
import numpy as np

CX = 8
NZ = 64
NY = 512
STEPS = 4
TR_DEV = 256
CAP = 16
CLUSTERS = 32
NX = 128
TRACES = 4096
N_GX = 16


def smooth_field(key, strength):
    height = strength * (0.9 + 0.2 * jax.random.uniform(key, (), jnp.float32))
    along_x = jnp.sin(math.pi * (jnp.arange(NX, dtype=jnp.float32) + 0.5) / NX)
    along_z = jnp.sin(math.pi * (jnp.arange(NZ, dtype=jnp.float32) + 0.5) / NZ)
    along_y = jnp.sin(math.pi * (jnp.arange(NY, dtype=jnp.float32) + 0.5) / NY)
    return height * along_x[:, None, None] * along_z[None, :, None] * along_y[None, None, :]


def draw_velocity(key, part):
    key = jax.random.fold_in(key, 5)
    fraction = jax.random.uniform(key, (NX, NZ, NY), jnp.float32)
    return 1.5 + 2.9 * fraction


def draw_adj_prev(key, part):
    common = smooth_field(key, 0.5)
    key = jax.random.fold_in(key, 21)
    jitter = jnp.clip(jax.random.normal(key, (NX, NZ, NY), jnp.float32), -6.0, 6.0)
    return common + jitter


def draw_adj_now(key, part):
    common = smooth_field(key, 0.5)
    key = jax.random.fold_in(key, 22)
    jitter = jnp.clip(jax.random.normal(key, (NX, NZ, NY), jnp.float32), -6.0, 6.0)
    return common + jitter


def touch_ends(entries, own_key, least, top_value):
    dims = entries.shape
    index_at = [jax.random.randint(jax.random.fold_in(own_key, axis), (), 0, dims[axis]) for axis in range(len(dims))]
    entries = entries.at[tuple(index_at)].set(least)
    longest = dims.index(max(dims))
    index_at[longest] = (index_at[longest] + 1) % dims[longest]
    return entries.at[tuple(index_at)].set(top_value)


def levels(own_key, extent, split, smallest, top_value):
    loudness, own = 1.0, jax.random.fold_in(own_key, 6)
    for position, shards_of in split:
        steps = jnp.exp(jax.random.uniform(jax.random.fold_in(own, position), (shards_of,), jnp.float32, smallest / len(split), top_value / len(split)))
        loudness = loudness * jnp.repeat(steps, extent[position] // shards_of).reshape([-1 if axis == position else 1 for axis in range(len(extent))])
    return loudness


def deal_out(key, own, number, rows, amount, top, most, lean):
    order = jax.random.permutation(key, amount)
    heavy_load, ordinary = shares(amount, rows * top, most, lean, True), shares(amount, rows * top, most, lean, False)
    places = jnp.arange(amount)

    def named(sizes, rotation):
        used = int((sizes > 0).sum())
        fixed = max(1, used // 4)
        passed = fixed + (places - fixed + rotation * (used - fixed)) % max(1, amount - fixed)
        return jnp.zeros((amount,), jnp.int32).at[order[jnp.where(places < fixed, places, passed)]].set(jnp.asarray(sizes, jnp.int32))

    sizes = jnp.where(number % 4 == 0, named(heavy_load, number // 4), named(ordinary, number - number // 4 - 1))
    mixed = jax.random.permutation(jax.random.fold_in(own, 3), amount)
    giver, taker = mixed[0:amount // 2 * 2:2], mixed[1:amount // 2 * 2:2]
    room = jnp.minimum(sizes[giver] - 1, most - sizes[taker]) // 2
    room = jnp.where((giver == order[0]) | (taker == order[0]) | (sizes[taker] == 0), 0, jnp.maximum(room, 0))
    passed = jax.random.randint(jax.random.fold_in(own, 4), (amount // 2,), 0, 1 << 20) % (room + 1)
    sizes = sizes.at[giver].add(-passed).at[taker].add(passed)
    labels = jnp.searchsorted(jnp.cumsum(sizes), jnp.arange(rows * top), side="right").astype(jnp.int32)
    table = labels.reshape(top, rows).T
    table = table[jax.random.permutation(jax.random.fold_in(own, 1), rows)]
    rotation = jax.random.randint(jax.random.fold_in(own, 2), (rows, 1), 0, top)
    return jnp.take_along_axis(table, (jnp.arange(top)[None, :] + rotation) % top, axis=1)


def shares(number_of, total, bound, skew, full):
    weights = [(1 << 20) // math.isqrt(rank ** skew) + 1 for rank in range(1, number_of + 1)]
    largest = bound if full else min(bound, max(-(-total // number_of), total * weights[0] // sum(weights)))
    least = 1 if total - largest >= number_of - 1 else 0
    counts, rest = [largest] + [least] * (number_of - 1), total - largest - least * (number_of - 1)
    while rest > 0:
        free = [i for i in range(1, number_of) if counts[i] < largest] or [i for i in range(1, number_of) if counts[i] < bound]
        pool, remaining = sum([weights[i] for i in free]), rest
        for i in free:
            extra = min(bound - counts[i], max(1, remaining * weights[i] // pool), rest)
            counts[i] = counts[i] + extra
            rest = rest - extra
    return np.array(counts)


def bell_draw(key, dims, width, limit, split=(), kind=jnp.bfloat16):
    values = width * jax.random.normal(key, dims, jnp.float32)
    if split:
        values = values * levels(key, dims, split, -0.22, 0.18)
    return jnp.clip(values, -limit, limit).astype(kind)


def setup_inputs(seed: int = 0, part: int = 0) -> dict:
    arg_keys = jax.random.split(jax.random.key(seed), 10)
    part_keys = jax.random.split(jax.random.fold_in(arg_keys[9], part), 10)
    fwd_fields = bell_draw(part_keys[0], (STEPS + 2, NX, NZ, NY), 1.0, 6.0, ((1, 16),), jnp.float32)
    velocity = draw_velocity(jax.random.fold_in(arg_keys[9], 71), part)
    adj_prev = draw_adj_prev(jax.random.fold_in(jax.random.fold_in(arg_keys[9], part), 71), part)
    adj_now = draw_adj_now(jax.random.fold_in(jax.random.fold_in(arg_keys[9], part), 71), part)
    residual = bell_draw(part_keys[4], (STEPS, TRACES), 1.0, 6.0, ((1, 16),), jnp.float32)
    rec_owner_keys = jax.random.split(jax.random.fold_in(arg_keys[5], 1), TRACES // TR_DEV)
    rec_owner_turns = jax.random.permutation(jax.random.fold_in(arg_keys[5], 3), TRACES // TR_DEV)
    rec_owner = jax.vmap(lambda own, number: deal_out(jax.random.fold_in(arg_keys[5], 2), own, number, TR_DEV, N_GX, 1, CAP, 2))(rec_owner_keys, rec_owner_turns).reshape((TRACES, 1))
    rec_cell = touch_ends(jax.random.randint(arg_keys[6], (TRACES,), 0, CX * NZ * NY), jax.random.fold_in(arg_keys[6], 1), 0, (CX * NZ * NY) - 1).astype(jnp.int32)
    rec_cluster = touch_ends(jax.random.randint(arg_keys[7], (TRACES,), 0, CLUSTERS), jax.random.fold_in(arg_keys[7], 1), 0, CLUSTERS - 1).astype(jnp.int32)
    cluster_gain = jnp.clip(jnp.exp(jax.random.uniform(arg_keys[8], (CLUSTERS,), jnp.float32, math.log(0.5), math.log(2.0))), 0.5, 2.0)
    return dict(fwd_fields=fwd_fields, velocity=velocity, adj_prev=adj_prev, adj_now=adj_now, residual=residual, rec_owner=rec_owner, rec_cell=rec_cell, rec_cluster=rec_cluster, cluster_gain=cluster_gain)


stencil_weights = (-205.0 / 72.0, 8.0 / 5.0, -1.0 / 5.0, 8.0 / 315.0, -1.0 / 560.0)
time_ratio = 0.1


def laplace(extended):
    row_count = extended.shape[0] - 8
    centre = extended[4:4 + row_count]
    depth_cells = centre.shape[1]
    cross_cells = centre.shape[2]
    summed = (3.0 * stencil_weights[0]) * centre
    for offset in range(1, 5):
        summed = summed + stencil_weights[offset] * (extended[4 + offset:4 + offset + row_count] + extended[4 - offset:4 - offset + row_count])
    padded_z = jnp.pad(centre, ((0, 0), (4, 4), (0, 0)))
    for offset in range(1, 5):
        summed = summed + stencil_weights[offset] * (padded_z[:, 4 + offset:4 + offset + depth_cells] + padded_z[:, 4 - offset:4 - offset + depth_cells])
    padded_y = jnp.pad(centre, ((0, 0), (0, 0), (4, 4)))
    for offset in range(1, 5):
        summed = summed + stencil_weights[offset] * (padded_y[:, :, 4 + offset:4 + offset + cross_cells] + padded_y[:, :, 4 - offset:4 - offset + cross_cells])
    return summed


def reference(fwd_fields, velocity, adj_prev, adj_now, residual, rec_owner, rec_cell, rec_cluster, cluster_gain):
    courant = jnp.square(time_ratio * velocity)
    scaling = 2.0 / velocity
    amplitude = residual * cluster_gain[rec_cluster][None, :]
    flat_index = (rec_owner[:, 0] * (CX * NZ * NY) + rec_cell).astype(jnp.int32)
    older = adj_prev
    newer = adj_now
    image = jnp.zeros_like(adj_now)
    for step in range(STEPS):
        image = image + scaling * newer * (fwd_fields[step] - 2.0 * fwd_fields[step + 1] + fwd_fields[step + 2])
        padded = jnp.pad(newer, ((4, 4), (0, 0), (0, 0)))
        following = 2.0 * newer - older + courant * laplace(padded)
        following = following.reshape(-1).at[flat_index].add(amplitude[step]).reshape(following.shape)
        older = newer
        newer = following
    return (older, newer, image)
```

```python
import functools

import jax
import jax.numpy as jnp
from jax import lax
from jax.experimental import pallas as pl
from jax.experimental.pallas import tpu as pltpu
from jax.sharding import PartitionSpec as P

STEPS = 4
CAP = 16
CHUNKS = 4
PAD = 8
HALO = 4
LANES = 128
FIELDS = 6
MESH = pl.DeviceIdType.MESH

stencil_weights = (-205.0 / 72.0, 8.0 / 5.0, -1.0 / 5.0, 8.0 / 315.0, -1.0 / 560.0)
time_ratio = 0.1


def iota(shape, dim):
    return lax.broadcasted_iota(jnp.int32, shape, dim)


def pack_traces(n, residual, owner, cell, cluster, gain, width):
    traces = residual.shape[1]
    clusters = gain.shape[0]
    picked = cluster == iota((clusters, traces), 0)
    gains = jnp.sum(jnp.where(picked, gain, 0.0), axis=0, keepdims=True)
    amplitude = residual * gains
    member = jnp.where(owner == iota((n, traces), 0), 1.0, 0.0)
    upper = jnp.where(iota((traces, traces), 0) <= iota((traces, traces), 1), 1.0, 0.0)
    ranked = jnp.dot(
        member.astype(jnp.bfloat16),
        upper.astype(jnp.bfloat16),
        preferred_element_type=jnp.float32,
    )
    slot = jnp.sum(member * (ranked - 1.0), axis=0, keepdims=True)
    row = cell // width
    column = cell - row * width
    lines = jnp.concatenate(
        [
            amplitude,
            row.astype(jnp.float32),
            column.astype(jnp.float32),
            slot,
            jnp.zeros((LANES - STEPS - 3, traces), jnp.float32),
        ],
        axis=0,
    )
    lines = lines.T
    lane = iota((traces, LANES), 1)
    spread = jnp.zeros((traces, LANES), jnp.float32)
    for field in range(FIELDS):
        spread = jnp.where(lane // CAP == field, lines[:, field : field + 1], spread)
    slots = lines[:, FIELDS : FIELDS + 1].astype(jnp.int32)
    spread = jnp.where(lane % CAP == slots, spread, 0.0)
    return jnp.dot(
        member, spread, precision=lax.Precision.HIGHEST, preferred_element_type=jnp.float32
    )


def kernel(
    n,
    fwd_hbm,
    velocity_hbm,
    prev_hbm,
    now_hbm,
    residual,
    owner,
    cell,
    cluster,
    gain,
    older_hbm,
    newer_hbm,
    image_hbm,
    field,
    fwd,
    velocity,
    image,
    added,
    outbox,
    inbox,
    row_hot,
    columns,
    parts,
    load_sem,
    out_sem,
    send_sem,
    recv_sem,
    mail_send,
    mail_recv,
):
    shot = lax.axis_index("shot")
    me = lax.axis_index("gx")
    layers, depth, width = now_hbm.shape
    rows = depth // CHUNKS
    slots = n * CAP

    barrier = pltpu.get_barrier_semaphore()

    @pl.loop(1, n)
    def _(i):
        pl.semaphore_signal(
            barrier, inc=1, device_id=(shot, lax.rem(me + i, n)), device_id_type=MESH
        )

    loads = [
        pltpu.make_async_copy(
            now_hbm, field.at[1, pl.ds(HALO, layers), pl.ds(PAD, depth), :], load_sem.at[0]
        ),
        pltpu.make_async_copy(
            prev_hbm, field.at[0, pl.ds(HALO, layers), pl.ds(PAD, depth), :], load_sem.at[1]
        ),
        pltpu.make_async_copy(velocity_hbm, velocity, load_sem.at[2]),
        pltpu.make_async_copy(fwd_hbm, fwd, load_sem.at[3]),
    ]
    pl.semaphore_wait(barrier, n - 1)

    def zone(chunk):
        return pl.ds(pl.multiple_of(PAD + chunk * rows, 8), rows)

    def halo_copy(level, chunk, side, first):
        start = 0 if side == 0 else layers - HALO
        if first:
            source = now_hbm.at[
                pl.ds(start, HALO), pl.ds(pl.multiple_of(chunk * rows, 8), rows), :
            ]
        else:
            source = field.at[level, pl.ds(HALO + start, HALO), zone(chunk), :]
        landing = HALO + layers if side == 0 else 0
        other = me - 1 if side == 0 else me + 1
        other = jnp.clip(other, 0, n - 1)
        return pltpu.make_async_remote_copy(
            src_ref=source,
            dst_ref=field.at[level, pl.ds(landing, HALO), zone(chunk), :],
            send_sem=send_sem.at[level, side, chunk],
            recv_sem=recv_sem.at[level, side, chunk],
            device_id=(shot, other),
            device_id_type=MESH,
        )

    has_left = me > 0
    has_right = me < n - 1

    def start_halo(level, chunk, first=False):
        @pl.when(has_left)
        def _():
            halo_copy(level, chunk, 0, first).start()

        @pl.when(has_right)
        def _():
            halo_copy(level, chunk, 1, first).start()

    for chunk in range(CHUNKS):
        start_halo(1, chunk, True)
    for load in loads:
        load.start()

    packed = pack_traces(
        n, residual[...], owner[...], cell[...], cluster[...], gain[...], width
    )
    for device in range(n):
        outbox[device] = packed[device : device + 1, :]

    def mail(i):
        other = lax.rem(me + i, n)
        return pltpu.make_async_remote_copy(
            src_ref=outbox.at[other],
            dst_ref=inbox.at[me],
            send_sem=mail_send.at[i],
            recv_sem=mail_recv.at[i],
            device_id=(shot, other),
            device_id_type=MESH,
        )

    def mail_from(i):
        other = lax.rem(me + n - i, n)
        return pltpu.make_async_remote_copy(
            src_ref=outbox.at[other],
            dst_ref=inbox.at[other],
            send_sem=mail_send.at[i],
            recv_sem=mail_recv.at[i],
            device_id=(shot, other),
            device_id_type=MESH,
        )

    @pl.loop(1, n)
    def _(i):
        mail(i).start()

    inbox[me] = outbox[me]

    blank = jnp.zeros((layers, PAD, width), jnp.float32)
    for level in range(1, STEPS + 1):
        field[level, pl.ds(HALO, layers), pl.ds(0, PAD), :] = blank
        field[level, pl.ds(HALO, layers), pl.ds(PAD + depth, PAD), :] = blank
    edge = jnp.zeros((HALO, depth, width), jnp.float32)

    @pl.when(jnp.logical_not(has_left))
    def _():
        @pl.loop(1, STEPS + 1)
        def _(level):
            field[level, pl.ds(0, HALO), pl.ds(PAD, depth), :] = edge

    @pl.when(jnp.logical_not(has_right))
    def _():
        @pl.loop(1, STEPS + 1)
        def _(level):
            field[level, pl.ds(HALO + layers, HALO), pl.ds(PAD, depth), :] = edge

    @pl.loop(1, n)
    def _(i):
        mail_from(i).wait_recv()

    arrived = jnp.concatenate(
        [jnp.broadcast_to(inbox[device], (CAP, LANES)) for device in range(n)], axis=0
    )
    lane = iota((slots, LANES), 1)
    own_slot = iota((slots, LANES), 0) % CAP

    def pick(number):
        chosen = jnp.where(lane == number * CAP + own_slot, arrived, 0.0)
        return jnp.sum(chosen, axis=1, keepdims=True)

    for step in range(STEPS):
        rest = pick(step)
        for part in range(3):
            piece = rest.astype(jnp.bfloat16).astype(jnp.float32)
            parts[step, :, part : part + 1] = piece
            rest = rest - piece
    target_row = jnp.broadcast_to(pick(STEPS), (slots, LANES)).T[0:1, :].astype(jnp.int32)
    row_hot[...] = jnp.where(target_row == iota((layers * depth, slots), 0), 1.0, 0.0).astype(
        jnp.bfloat16
    )
    columns[...] = jnp.broadcast_to(pick(STEPS + 1), (slots, LANES)).astype(jnp.int32)

    for load in loads:
        load.wait()

    centre_weight = 3.0 * stencil_weights[0]

    @pl.loop(0, STEPS)
    def _(step):
        level = step + 1
        total = None
        hit = columns[:, 0:1] == iota((slots, width), 1)
        for part in range(3):
            values = jnp.where(hit, parts[step, :, part : part + 1], 0.0).astype(jnp.bfloat16)
            product = jnp.dot(row_hot[...], values, preferred_element_type=jnp.float32)
            total = product if total is None else total + product
        added[...] = total

        @pl.loop(0, CHUNKS)
        def _(chunk):
            here = zone(chunk)
            plain = pl.ds(pl.multiple_of(chunk * rows, 8), rows)
            window = pl.ds(pl.multiple_of(chunk * rows, 8), rows + 2 * PAD)

            @pl.when(has_left)
            def _():
                halo_copy(level, chunk, 1, False).wait_recv()

            @pl.when(has_right)
            def _():
                halo_copy(level, chunk, 0, False).wait_recv()

            lane = iota((rows, width), 1)

            @pl.loop(0, layers)
            def _(x):
                place = x + HALO
                strip = field[level, place, window, :]
                centre = strip[PAD : PAD + rows]
                summed = centre_weight * centre
                for m in range(1, 5):
                    pair = field[level, place + m, here, :] + field[level, place - m, here, :]
                    pair = pair + strip[PAD + m : PAD + m + rows] + strip[PAD - m : PAD - m + rows]
                    pair = pair + jnp.where(lane >= m, pltpu.roll(centre, m, 1), 0.0)
                    pair = pair + jnp.where(
                        lane < width - m, pltpu.roll(centre, width - m, 1), 0.0
                    )
                    summed = summed + stencil_weights[m] * pair
                speed = time_ratio * velocity[x, plain, :]
                following = 2.0 * centre - field[level - 1, place, here, :]
                following = following + (speed * speed) * summed
                following = following + added[
                    pl.ds(pl.multiple_of(x * depth + chunk * rows, 8), rows), :
                ]
                field[level + 1, place, here, :] = following
                change = (
                    fwd[step, x, plain, :]
                    - 2.0 * fwd[step + 1, x, plain, :]
                    + fwd[step + 2, x, plain, :]
                )
                term = centre * change

                @pl.when(step == 0)
                def _():
                    image[x, plain, :] = term

                @pl.when(step > 0)
                def _():
                    image[x, plain, :] = image[x, plain, :] + term

            @pl.when(step < STEPS - 1)
            def _():
                start_halo(level + 1, chunk)

    own = pl.ds(HALO, layers)
    inner = pl.ds(PAD, depth)
    stores = [
        pltpu.make_async_copy(field.at[STEPS, own, inner, :], older_hbm, out_sem.at[0]),
        pltpu.make_async_copy(field.at[STEPS + 1, own, inner, :], newer_hbm, out_sem.at[1]),
        pltpu.make_async_copy(image, image_hbm, out_sem.at[2]),
    ]
    for store in stores:
        store.start()

    @pl.loop(1, n)
    def _(i):
        mail(i).wait_send()

    def wait_halo(level, chunk, first):
        @pl.when(has_left)
        def _():
            halo_copy(level, chunk, 0, first).wait_send()

        @pl.when(has_right)
        def _():
            halo_copy(level, chunk, 1, first).wait_send()

    for chunk in range(CHUNKS):
        wait_halo(1, chunk, True)

    @pl.loop(2, STEPS + 1)
    def _(level):
        @pl.loop(0, CHUNKS)
        def _(chunk):
            wait_halo(level, chunk, False)

    for store in stores:
        store.wait()


def per_device(
    fwd_fields,
    velocity,
    adj_prev,
    adj_now,
    residual,
    rec_owner,
    rec_cell,
    rec_cluster,
    cluster_gain,
):
    n = lax.axis_size("gx")
    layers, depth, width = adj_now.shape
    traces = residual.shape[1]
    slots = n * CAP
    clusters = cluster_gain.shape[0]
    block = jax.ShapeDtypeStruct(adj_now.shape, jnp.float32)
    hbm = pl.BlockSpec(memory_space=pl.ANY)
    vmem = pl.BlockSpec(memory_space=pltpu.VMEM)
    older, newer, image = pl.pallas_call(
        functools.partial(kernel, n),
        out_shape=(block, block, block),
        in_specs=[hbm] * 4 + [vmem] * 5,
        out_specs=(hbm, hbm, hbm),
        scratch_shapes=[
            pltpu.VMEM(
                (STEPS + 2, layers + 2 * HALO, depth + 2 * PAD, width), jnp.float32
            ),
            pltpu.VMEM(fwd_fields.shape, jnp.float32),
            pltpu.VMEM(velocity.shape, jnp.float32),
            pltpu.VMEM(adj_now.shape, jnp.float32),
            pltpu.VMEM((layers * depth, width), jnp.float32),
            pltpu.VMEM((n, 1, LANES), jnp.float32),
            pltpu.VMEM((n, 1, LANES), jnp.float32),
            pltpu.VMEM((layers * depth, slots), jnp.bfloat16),
            pltpu.VMEM((slots, LANES), jnp.int32),
            pltpu.VMEM((STEPS, slots, LANES), jnp.float32),
            pltpu.SemaphoreType.DMA((4,)),
            pltpu.SemaphoreType.DMA((3,)),
            pltpu.SemaphoreType.DMA((STEPS + 1, 2, CHUNKS)),
            pltpu.SemaphoreType.DMA((STEPS + 1, 2, CHUNKS)),
            pltpu.SemaphoreType.DMA((n,)),
            pltpu.SemaphoreType.DMA((n,)),
        ],
        compiler_params=pltpu.CompilerParams(
            collective_id=0, has_side_effects=True, vmem_limit_bytes=48 * 1024 * 1024
        ),
        name="adjoint",
    )(
        fwd_fields,
        velocity,
        adj_prev,
        adj_now,
        residual,
        rec_owner.reshape(1, traces),
        rec_cell.reshape(1, traces),
        rec_cluster.reshape(1, traces),
        cluster_gain.reshape(clusters, 1),
    )
    return (older, newer, (2.0 / velocity) * image)


def solution(mesh):
    in_specs = (
        P(None, ("shot", "gx"), None, None),
        P("gx", None, None),
        P(("shot", "gx"), None, None),
        P(("shot", "gx"), None, None),
        P(None, ("shot", "gx")),
        P("gx", None),
        P("gx"),
        P("gx"),
        P(),
    )
    out_specs = (
        P(("shot", "gx"), None, None),
        P(("shot", "gx"), None, None),
        P(("shot", "gx"), None, None),
    )
    return jax.shard_map(
        per_device, mesh=mesh, in_specs=in_specs, out_specs=out_specs, check_vma=False
    )
```

```python
import functools

import jax
import jax.numpy as jnp
from jax import lax
from jax.experimental import pallas as pl
from jax.experimental.pallas import tpu as pltpu
from jax.sharding import PartitionSpec as P

STEPS = 4
CAP = 16
CHUNKS = 4
PIECES = 3
PAD = 8
HALO = 4
LANES = 128
FIELDS = 6
VMEM_BYTES = 62 * 1024 * 1024
MESH = pl.DeviceIdType.MESH

stencil_weights = (-205.0 / 72.0, 8.0 / 5.0, -1.0 / 5.0, 8.0 / 315.0, -1.0 / 560.0)
time_ratio = 0.1


def iota(shape, dim):
    return lax.broadcasted_iota(jnp.int32, shape, dim)


def pack_traces(n, residual, owner, cell, cluster, gain, width):
    traces = residual.shape[1]
    clusters = gain.shape[1]
    square = (clusters, clusters)
    gain = jnp.where(iota(square, 0) == iota(square, 1), gain, 0.0)
    gain = jnp.sum(gain, axis=1, keepdims=True)
    picked = cluster == iota((clusters, traces), 0)
    gains = jnp.sum(jnp.where(picked, gain, 0.0), axis=0, keepdims=True)
    amplitude = residual * gains
    member = jnp.where(owner == iota((n, traces), 0), 1.0, 0.0)
    upper = jnp.where(iota((traces, traces), 0) <= iota((traces, traces), 1), 1.0, 0.0)
    ranked = jnp.dot(
        member.astype(jnp.bfloat16),
        upper.astype(jnp.bfloat16),
        preferred_element_type=jnp.float32,
    )
    slot = jnp.sum(member * (ranked - 1.0), axis=0, keepdims=True)
    row = cell // width
    column = cell - row * width
    lines = jnp.concatenate(
        [
            amplitude,
            row.astype(jnp.float32),
            column.astype(jnp.float32),
            slot,
            jnp.zeros((LANES - STEPS - 3, traces), jnp.float32),
        ],
        axis=0,
    )
    lines = lines.T
    lane = iota((traces, LANES), 1)
    spread = jnp.zeros((traces, LANES), jnp.float32)
    for field in range(FIELDS):
        spread = jnp.where(lane // CAP == field, lines[:, field : field + 1], spread)
    slots = lines[:, FIELDS : FIELDS + 1].astype(jnp.int32)
    spread = jnp.where(lane % CAP == slots, spread, 0.0)
    return jnp.dot(
        member, spread, precision=lax.Precision.HIGHEST, preferred_element_type=jnp.float32
    )


def kernel(
    n,
    fwd_hbm,
    velocity_hbm,
    prev_hbm,
    now_hbm,
    residual_hbm,
    owner_hbm,
    cell_hbm,
    cluster_hbm,
    gain_hbm,
    older_hbm,
    newer_hbm,
    image_hbm,
    field,
    fwd,
    velocity,
    image,
    added,
    outbox,
    inbox,
    row_hot,
    columns,
    parts,
    band,
    residual,
    owner,
    cell,
    cluster,
    gain,
    load_sem,
    out_sem,
    send_sem,
    recv_sem,
    mail_send,
    mail_recv,
):
    shot = lax.axis_index("shot")
    me = lax.axis_index("gx")
    layers, depth, width = now_hbm.shape
    rows = depth // CHUNKS
    slots = n * CAP

    barrier = pltpu.get_barrier_semaphore()

    @pl.loop(1, n)
    def _(i):
        pl.semaphore_signal(
            barrier, inc=1, device_id=(shot, lax.rem(me + i, n)), device_id_type=MESH
        )

    tables = [
        pltpu.make_async_copy(residual_hbm, residual, load_sem.at[4]),
        pltpu.make_async_copy(owner_hbm, owner, load_sem.at[5]),
        pltpu.make_async_copy(cell_hbm, cell, load_sem.at[6]),
        pltpu.make_async_copy(cluster_hbm, cluster, load_sem.at[7]),
        pltpu.make_async_copy(gain_hbm, gain, load_sem.at[8]),
    ]
    loads = [
        pltpu.make_async_copy(
            now_hbm, field.at[1, pl.ds(HALO, layers), pl.ds(PAD, depth), :], load_sem.at[0]
        ),
        pltpu.make_async_copy(
            prev_hbm, field.at[0, pl.ds(HALO, layers), pl.ds(PAD, depth), :], load_sem.at[1]
        ),
        pltpu.make_async_copy(velocity_hbm, velocity, load_sem.at[2]),
        pltpu.make_async_copy(fwd_hbm, fwd, load_sem.at[3]),
    ]
    for load in tables + loads:
        load.start()
    for load in tables:
        load.wait()

    packed = pack_traces(
        n, residual[...], owner[...], cell[...], cluster[...], gain[...], width
    )
    for device in range(n):
        outbox[device] = packed[device : device + 1, :]

    pl.semaphore_wait(barrier, n - 1)

    def zone(chunk):
        return pl.ds(pl.multiple_of(PAD + chunk * rows, 8), rows)

    def halo_copy(level, chunk, side, first):
        start = 0 if side == 0 else layers - HALO
        if first:
            source = now_hbm.at[
                pl.ds(start, HALO), pl.ds(pl.multiple_of(chunk * rows, 8), rows), :
            ]
        else:
            source = field.at[level, pl.ds(HALO + start, HALO), zone(chunk), :]
        landing = HALO + layers if side == 0 else 0
        other = me - 1 if side == 0 else me + 1
        other = jnp.clip(other, 0, n - 1)
        return pltpu.make_async_remote_copy(
            src_ref=source,
            dst_ref=field.at[level, pl.ds(landing, HALO), zone(chunk), :],
            send_sem=send_sem.at[level, side, chunk],
            recv_sem=recv_sem.at[level, side, chunk],
            device_id=(shot, other),
            device_id_type=MESH,
        )

    has_left = me > 0
    has_right = me < n - 1

    def start_halo(level, chunk, first=False):
        @pl.when(has_left)
        def _():
            halo_copy(level, chunk, 0, first).start()

        @pl.when(has_right)
        def _():
            halo_copy(level, chunk, 1, first).start()

    def wait_halo(level, chunk, first=False):
        @pl.when(has_left)
        def _():
            halo_copy(level, chunk, 0, first).wait_send()

        @pl.when(has_right)
        def _():
            halo_copy(level, chunk, 1, first).wait_send()

    def mail(i):
        other = lax.rem(me + i, n)
        return pltpu.make_async_remote_copy(
            src_ref=outbox.at[other],
            dst_ref=inbox.at[me],
            send_sem=mail_send.at[i],
            recv_sem=mail_recv.at[i],
            device_id=(shot, other),
            device_id_type=MESH,
        )

    def mail_from(i):
        other = lax.rem(me + n - i, n)
        return pltpu.make_async_remote_copy(
            src_ref=outbox.at[other],
            dst_ref=inbox.at[other],
            send_sem=mail_send.at[i],
            recv_sem=mail_recv.at[i],
            device_id=(shot, other),
            device_id_type=MESH,
        )

    @pl.loop(1, n)
    def _(i):
        mail(i).start()

    inbox[me] = outbox[me]
    for chunk in range(0, CHUNKS):
        start_halo(1, chunk, True)


    image[...] = jnp.zeros_like(image)
    apart = jnp.abs(iota((width, width), 0) - iota((width, width), 1))
    weights = jnp.zeros((width, width), jnp.float32)
    for m, whole in ((1, 8064.0), (2, -1008.0), (3, 128.0), (4, -9.0)):
        weights = jnp.where(apart == m, whole, weights)
    band[...] = weights.astype(jnp.bfloat16)
    blank = jnp.zeros((layers, PAD, width), jnp.float32)
    for level in range(1, STEPS + 1):
        field[level, pl.ds(HALO, layers), pl.ds(0, PAD), :] = blank
        field[level, pl.ds(HALO, layers), pl.ds(PAD + depth, PAD), :] = blank
    edge = jnp.zeros((HALO, depth, width), jnp.float32)

    @pl.when(jnp.logical_not(has_left))
    def _():
        @pl.loop(1, STEPS + 1)
        def _(level):
            field[level, pl.ds(0, HALO), pl.ds(PAD, depth), :] = edge

    @pl.when(jnp.logical_not(has_right))
    def _():
        @pl.loop(1, STEPS + 1)
        def _(level):
            field[level, pl.ds(HALO + layers, HALO), pl.ds(PAD, depth), :] = edge

    @pl.loop(1, n)
    def _(i):
        mail_from(i).wait_recv()

    arrived = jnp.concatenate(
        [jnp.broadcast_to(inbox[device], (CAP, LANES)) for device in range(n)], axis=0
    )
    lane = iota((slots, LANES), 1)
    own_slot = iota((slots, LANES), 0) % CAP

    def pick(number):
        chosen = jnp.where(lane == number * CAP + own_slot, arrived, 0.0)
        return jnp.sum(chosen, axis=1, keepdims=True)

    for step in range(STEPS):
        rest = pick(step)
        for part in range(3):
            piece = rest.astype(jnp.bfloat16).astype(jnp.float32)
            parts[step, :, part : part + 1] = piece
            rest = rest - piece
    target_row = jnp.broadcast_to(pick(STEPS), (slots, LANES)).T[0:1, :].astype(jnp.int32)
    row_hot[...] = jnp.where(target_row == iota((layers * depth, slots), 0), 1.0, 0.0).astype(
        jnp.bfloat16
    )
    columns[...] = jnp.broadcast_to(pick(STEPS + 1), (slots, LANES)).astype(jnp.int32)

    for load in loads:
        load.wait()

    centre_weight = 3.0 * stencil_weights[0]
    y_scale = 1.0 / 5040.0

    def sum_traces(step):
        total = None
        hit = columns[:, 0:1] == iota((slots, width), 1)
        for part in range(3):
            values = jnp.where(hit, parts[step, :, part : part + 1], 0.0).astype(jnp.bfloat16)
            product = jnp.dot(row_hot[...], values, preferred_element_type=jnp.float32)
            total = product if total is None else total + product
        added[step % 2] = total

    sum_traces(0)

    @pl.loop(0, STEPS)
    def _(step):
        level = step + 1
        @pl.loop(0, CHUNKS)
        def _(chunk):
            here = zone(chunk)
            plain = pl.ds(pl.multiple_of(chunk * rows, 8), rows)
            window = pl.ds(pl.multiple_of(chunk * rows, 8), rows + 2 * PAD)

            @pl.when(has_left)
            def _():
                halo_copy(level, chunk, 1, False).wait_recv()

            @pl.when(has_right)
            def _():
                halo_copy(level, chunk, 0, False).wait_recv()

            rest = field[level, pl.ds(HALO, layers), here, :].reshape(layers * rows, width)
            across = None
            for part in range(PIECES):
                piece = rest.astype(jnp.bfloat16)
                product = jnp.dot(piece, band[...], preferred_element_type=jnp.float32)
                across = product if across is None else across + product
                rest = rest - piece.astype(jnp.float32)

            for x in range(layers):
                place = x + HALO
                strip = field[level, place, window, :]
                centre = strip[PAD : PAD + rows]
                summed = centre_weight * centre + y_scale * across[x * rows : (x + 1) * rows]
                for m in range(1, 5):
                    pair = field[level, place + m, here, :] + field[level, place - m, here, :]
                    pair = pair + strip[PAD + m : PAD + m + rows] + strip[PAD - m : PAD - m + rows]
                    summed = summed + stencil_weights[m] * pair
                speed = time_ratio * velocity[x, plain, :]
                following = 2.0 * centre - field[level - 1, place, here, :]
                following = following + (speed * speed) * summed
                following = following + added[
                    step % 2, pl.ds(pl.multiple_of(x * depth + chunk * rows, 8), rows), :
                ]
                field[level + 1, place, here, :] = following
                change = (
                    fwd[step, x, plain, :]
                    - 2.0 * fwd[step + 1, x, plain, :]
                    + fwd[step + 2, x, plain, :]
                )
                term = centre * change

                image[x, plain, :] = image[x, plain, :] + term

            @pl.when(step < STEPS - 1)
            def _():
                start_halo(level + 1, chunk)

            @pl.when(jnp.logical_and(step < STEPS - 1, chunk == 1))
            def _():
                sum_traces(step + 1)

    own = pl.ds(HALO, layers)
    inner = pl.ds(PAD, depth)
    stores = [
        pltpu.make_async_copy(field.at[STEPS, own, inner, :], older_hbm, out_sem.at[0]),
        pltpu.make_async_copy(field.at[STEPS + 1, own, inner, :], newer_hbm, out_sem.at[1]),
        pltpu.make_async_copy(image, image_hbm, out_sem.at[2]),
    ]
    for store in stores:
        store.start()

    @pl.loop(1, n)
    def _(i):
        mail(i).wait_send()

    for chunk in range(0, CHUNKS):
        wait_halo(1, chunk, True)

    @pl.loop(2, STEPS + 1)
    def _(level):
        @pl.loop(0, CHUNKS)
        def _(chunk):
            wait_halo(level, chunk)

    for store in stores:
        store.wait()


def per_device(
    fwd_fields,
    velocity,
    adj_prev,
    adj_now,
    residual,
    rec_owner,
    rec_cell,
    rec_cluster,
    cluster_gain,
):
    n = lax.axis_size("gx")
    width = adj_now.shape[2]
    layers, depth = adj_now.shape[:2]
    traces = residual.shape[1]
    slots = n * CAP
    clusters = cluster_gain.shape[0]
    block = jax.ShapeDtypeStruct(adj_now.shape, jnp.float32)
    hbm = pl.BlockSpec(memory_space=pltpu.HBM)
    older, newer, image = pl.pallas_call(
        functools.partial(kernel, n),
        out_shape=(block, block, block),
        in_specs=[hbm] * 9,
        out_specs=(hbm, hbm, hbm),
        scratch_shapes=[
            pltpu.VMEM(
                (STEPS + 2, layers + 2 * HALO, depth + 2 * PAD, width), jnp.float32
            ),
            pltpu.VMEM(fwd_fields.shape, jnp.float32),
            pltpu.VMEM(velocity.shape, jnp.float32),
            pltpu.VMEM(adj_now.shape, jnp.float32),
            pltpu.VMEM((2, layers * depth, width), jnp.float32),
            pltpu.VMEM((n, 1, LANES), jnp.float32),
            pltpu.VMEM((n, 1, LANES), jnp.float32),
            pltpu.VMEM((layers * depth, slots), jnp.bfloat16),
            pltpu.VMEM((slots, LANES), jnp.int32),
            pltpu.VMEM((STEPS, slots, LANES), jnp.float32),
            pltpu.VMEM((width, width), jnp.bfloat16),
            pltpu.VMEM(residual.shape, jnp.float32),
            pltpu.VMEM((1, traces), jnp.int32),
            pltpu.VMEM((1, traces), jnp.int32),
            pltpu.VMEM((1, traces), jnp.int32),
            pltpu.VMEM((1, clusters), jnp.float32),
            pltpu.SemaphoreType.DMA((9,)),
            pltpu.SemaphoreType.DMA((3,)),
            pltpu.SemaphoreType.DMA((STEPS + 1, 2, CHUNKS)),
            pltpu.SemaphoreType.DMA((STEPS + 1, 2, CHUNKS)),
            pltpu.SemaphoreType.DMA((n,)),
            pltpu.SemaphoreType.DMA((n,)),
        ],
        compiler_params=pltpu.CompilerParams(
            collective_id=0, has_side_effects=True, vmem_limit_bytes=VMEM_BYTES
        ),
        name="adjoint",
    )(
        fwd_fields,
        velocity,
        adj_prev,
        adj_now,
        residual,
        rec_owner.reshape(1, traces),
        rec_cell.reshape(1, traces),
        rec_cluster.reshape(1, traces),
        cluster_gain.reshape(1, clusters),
    )
    return (older, newer, (2.0 / velocity) * image)


def solution(mesh):
    in_specs = (
        P(None, ("shot", "gx"), None, None),
        P("gx", None, None),
        P(("shot", "gx"), None, None),
        P(("shot", "gx"), None, None),
        P(None, ("shot", "gx")),
        P("gx", None),
        P("gx"),
        P("gx"),
        P(),
    )
    out_specs = (
        P(("shot", "gx"), None, None),
        P(("shot", "gx"), None, None),
        P(("shot", "gx"), None, None),
    )
    return jax.shard_map(
        per_device, mesh=mesh, in_specs=in_specs, out_specs=out_specs, check_vma=False
    )
```
